128 devices in a mesh: team: 16 (over x_hi, z, core), tile: 8 (over y, x_lo).
Axes of the slice: x: 4 (x_hi: 2, x_lo: 2; x = x_hi * 2 + x_lo), y: 4, z: 4, core: 2. Of those that a mesh axis runs over, the one named last changes fastest.
Arguments:
- points: float32 [8, 131072], P(None, ('team', 'tile')), may hold values from -6 to 6
- scales: float32 [8], replicated, may hold values from 1.2 to 3
- vectors: float32 [16, 131072], P(None, ('team', 'tile')), may hold values from -6 to 6
- plan: int32 [2], replicated, may hold values from 1 to 15, as said below
Outputs:
- smoothed: float32 [16, 131072], P(None, ('team', 'tile'))
The draws below stay inside these ranges and needn't reach their ends.
Inputs may be any that keep to these rules, and one draw needn't show every extreme that they name: `plan`: the 2 values are distinct; one of them is 15.
All inputs are finite; a program needn't handle non-finite values.
Results may differ from the reference program's by a relative error of at most 0.00084.
Values sent between devices are 32-bit elements; how exact they have to be, the bound alone decides.
A program may use at most 64 MiB of HBM per device.

```python
import math
import jax
import jax.numpy as jnp
from jax import lax

DIM = 8
RHS = 16
ROUNDS = 2
BLOCK = 8192
NBLK = 16
POINTS = 131072


def draw_plan(key, part):
    key = jax.random.fold_in(key, 7)
    first_key, second_key = jax.random.split(key)
    another = jax.random.randint(first_key, (), 1, NBLK - 1)
    flipped = jax.random.randint(second_key, (), 0, 2)
    farthest = jnp.full((), NBLK - 1, jnp.int32)
    return jnp.where(flipped == 1, jnp.stack([another, farthest]), jnp.stack([farthest, another])).astype(jnp.int32)


def shard_levels(stream_key, shape, shards, smallest, top_value):
    loudness = 1.0
    for dim, blocks in shards:
        draws = jax.random.uniform(jax.random.fold_in(jax.random.fold_in(stream_key, 6), dim), (blocks,), jnp.float32, smallest / len(shards), top_value / len(shards))
        loudness = loudness * jnp.repeat(jnp.exp(draws), shape[dim] // blocks).reshape((-1,) + (1,) * (len(shape) - 1 - dim))
    return loudness


def noise(own_key, dims, scale, reach, cuts=(), held_as=jnp.bfloat16):
    gain = shard_levels(own_key, dims, cuts, -0.22, 0.18) if cuts else 1.0
    drawn = jax.random.normal(own_key, dims, jnp.float32) * scale * gain
    return jnp.minimum(jnp.maximum(drawn, -reach), reach).astype(held_as)


def setup_inputs(seed: int = 0) -> dict:
    splits = jax.random.split(jax.random.key(seed), 5)
    return {
        "points": noise(splits[0], (DIM, POINTS), 1.0, 6.0, ((1, 128),), jnp.float32),
        "scales": jnp.clip(jnp.exp(jax.random.uniform(splits[1], (DIM,), jnp.float32, math.log(1.2), math.log(3.0))), 1.2, 3.0),
        "vectors": noise(splits[2], (RHS, POINTS), 1.0, 6.0, ((1, 128),), jnp.float32),
        "plan": draw_plan(jax.random.fold_in(splits[4], 71), 0),
    }


amplitude = 0.03
jitter = 0.5
sqrt_five = math.sqrt(5.0)

def kernel_part(row_x, col_x):
    squared = jnp.zeros((row_x.shape[1], col_x.shape[1]), jnp.float32)
    for coord in range(row_x.shape[0]):
        difference = row_x[coord][:, None] - col_x[coord][None, :]
        squared = squared + difference * difference
    distance = jnp.sqrt(squared)
    value = amplitude * (1.0 + sqrt_five * distance + 5.0 / 3.0 * squared) * jnp.exp(-sqrt_five * distance)
    return value.astype(jnp.bfloat16)

def block_width(col_total):
    col_width = 1
    while col_width * 2 <= 2048 and col_total % (col_width * 2) == 0:
        col_width = col_width * 2
    return col_width

def sweep(row_x, col_x, col_v):
    col_total = col_x.shape[1]
    col_width = block_width(col_total)
    block_count = col_total // col_width
    blocks_x = col_x.reshape(col_x.shape[0], block_count, col_width).transpose(1, 0, 2)
    blocks_v = col_v.reshape(col_v.shape[0], block_count, col_width).transpose(1, 0, 2)

    def advance(running, pieces):
        piece_x, piece_v = pieces
        part = kernel_part(row_x, piece_x)
        running = running + lax.dot_general(piece_v, part, (((1,), (1,)), ((), ())), preferred_element_type=jnp.float32)
        return (running, None)
    start_acc = jnp.zeros((col_v.shape[0], row_x.shape[1]), jnp.float32)
    summed, unused = lax.scan(advance, start_acc, (blocks_x, blocks_v))
    return summed

def reference(points, scales, vectors, plan):
    scaled = points / scales[:, None]
    vecbf = vectors.astype(jnp.bfloat16)

    def one_block(block_no):
        rows_x = lax.dynamic_slice_in_dim(scaled, (block_no * BLOCK).astype(jnp.int32), BLOCK, 1)
        summed = jnp.zeros((vectors.shape[0], BLOCK), jnp.float32)
        partners = [block_no] + [jnp.bitwise_xor(block_no, plan[match_no]).astype(jnp.int32) for match_no in range(ROUNDS)]
        for partner in partners:
            first = (partner * BLOCK).astype(jnp.int32)
            cols_x = lax.dynamic_slice_in_dim(scaled, first, BLOCK, 1)
            cols_v = lax.dynamic_slice_in_dim(vecbf, first, BLOCK, 1)
            summed = summed + sweep(rows_x, cols_x, cols_v)
        return summed
    blocks = lax.map(one_block, jnp.arange(NBLK, dtype=jnp.int32))
    products = blocks.transpose(1, 0, 2).reshape(vectors.shape)
    return jitter * vectors + products
```

```python
import functools
import math

import jax
import jax.numpy as jnp
from jax import lax
from jax.experimental import pallas as pl
from jax.experimental.pallas import tpu as pltpu
from jax.sharding import PartitionSpec as P

MESH = pl.DeviceIdType.MESH
VMEM = pltpu.VMEM
F32 = jnp.float32
BF16 = jnp.bfloat16

SHRINK = math.sqrt(0.05)
RATE = -10.0 / math.log(2.0)
COORDS = 8
RHS = 16
DEPTH = 64
UNIT = 512
HOPS = 4
PER_ROW = 17


def tile_id(offset):
    count = lax.axis_size("tile")
    return {"tile": lax.rem(lax.axis_index("tile") + offset + count, count)}


def team_id(pairing):
    me = lax.axis_index("team")
    bits = lax.axis_size("team").bit_length() - 1
    other = me * 0
    for bit in range(bits):
        mine = lax.rem(me // (1 << bit), 2)
        other = other + (1 << bit) * (1 - mine if pairing >> bit & 1 else mine)
    return {"team": other}


def greet():
    barrier = pltpu.get_barrier_semaphore()
    tiles = lax.axis_size("tile")
    teams = lax.axis_size("team")
    friends = [tile_id(step) for step in range(1, tiles)]
    friends += [team_id(1 << bit) for bit in range(teams.bit_length() - 1)]
    friends.append(team_id(teams - 1))
    for friend in friends:
        pl.semaphore_signal(barrier, inc=1, device_id=friend, device_id_type=MESH)
    pl.semaphore_wait(barrier, len(friends))


def remote(src, dst, send, recv, target):
    return pltpu.make_async_remote_copy(
        src_ref=src, dst_ref=dst, send_sem=send, recv_sem=recv, device_id=target, device_id_type=MESH
    )


def chosen(plan_ref, bit, arrived, held):
    pairing = plan_ref[0] + plan_ref[1] - 15
    taken = jnp.bitwise_and(jnp.right_shift(pairing, bit), 1).astype(F32)
    mask = jnp.full(held.shape, taken, F32) > 0.5
    return jnp.where(mask, arrived, held)


def fetch_kernel(plan_ref, own_ref, cols_ref, far_ref, near_ref, held, got, sends, recvs):
    greet()
    copies = []
    for hop in range(1, HOPS + 1):
        copies.append(remote(own_ref, cols_ref.at[hop - 1], sends.at[hop - 1], recvs.at[hop - 1], tile_id(-hop)))
    copies.append(remote(own_ref, far_ref, sends.at[4], recvs.at[4], team_id(15)))
    for copy in copies:
        copy.start()
    for bit in range(4):
        src = own_ref if bit == 0 else held.at[bit - 1]
        copy = remote(src, got.at[bit], sends.at[5 + bit], recvs.at[5 + bit], team_id(1 << bit))
        copy.start()
        copy.wait()
        value = chosen(plan_ref, bit, got[bit], src[...])
        if bit < 3:
            held[bit] = value
        else:
            near_ref[...] = value
    for copy in copies:
        copy.wait()


def give_kernel(plan_ref, vec_ref, rows_ref, cols_ref, out_ref, back, far, held, got, sends, recvs):
    greet()
    size = vec_ref.shape[1]
    copies = []
    for hop in range(1, HOPS + 1):
        src = cols_ref.at[hop]
        copies.append(remote(src, back.at[hop - 1], sends.at[hop - 1], recvs.at[hop - 1], tile_id(hop)))
    copies.append(remote(rows_ref.at[1], far, sends.at[4], recvs.at[4], team_id(15)))
    for copy in copies:
        copy.start()
    total = 0.5 * vec_ref[...] + rows_ref[0] + cols_ref[0]
    for bit in range(4):
        src = rows_ref.at[2] if bit == 0 else held.at[bit - 1]
        copy = remote(src, got.at[bit], sends.at[5 + bit], recvs.at[5 + bit], team_id(1 << bit))
        copy.start()
        copy.wait()
        value = chosen(plan_ref, bit, got[bit], src[...])
        if bit < 3:
            held[bit] = value
        else:
            total = total + value
    for copy in copies:
        copy.wait()
    total = total + far[...]
    for hop in range(HOPS):
        total = total + back[hop]
    out_ref[...] = total


def pieces(value, count):
    out = []
    for _ in range(count):
        piece = value.astype(BF16).astype(F32)
        out.append(piece)
        value = value - piece
    return out


def split(shard, scales):
    scaled = shard[:COORDS] / scales * SHRINK
    one, two, three = pieces(scaled, 3)
    norm = jnp.sum(scaled * scaled, axis=0, keepdims=True)
    return one, two, three, pieces(norm, 3)


def place(parts, size):
    row = lax.broadcasted_iota(jnp.int32, (8, size), 0)
    out = jnp.zeros((8, size), F32)
    for at, part in enumerate(parts):
        out = jnp.where(row == at, part, out)
    return out


def col_operand(shard, scales):
    one, two, three, norms = split(shard, scales)
    unit = jnp.ones_like(norms[0])
    tail = place(norms + [unit] * 3, shard.shape[1])
    return jnp.concatenate([one, one, one, two, two, three, tail, jnp.zeros_like(tail)], 0).astype(BF16)


def row_operand(shard, scales):
    one, two, three, norms = split(shard, scales)
    unit = jnp.ones_like(norms[0])
    tail = place([unit] * 3 + norms, shard.shape[1])
    stack = [-2.0 * one, -2.0 * two, -2.0 * three, -2.0 * one, -2.0 * two, -2.0 * one, tail]
    stack += [jnp.zeros_like(tail)] * 9
    return jnp.concatenate(stack, 0).T


def matern(small):
    small = jnp.maximum(small, 1e-30)
    w = small * lax.rsqrt(small)
    return ((w * (w + 0.3) + 0.03) * jnp.exp2(w * RATE)).astype(BF16)


def pair_kernel(
    scales_ref, own_ref, cols_ref, far_ref, near_ref, rows_out, cols_out, small, work, col_x, col_v, row_v, acc_r, acc_c
):
    size = own_ref.shape[1]
    halves = size // UNIT
    units = 3 * PER_ROW
    scales = scales_ref[...]
    for row, ref in enumerate((own_ref, far_ref, near_ref)):
        shard = ref[...]
        work[2 * UNIT + row * size : 2 * UNIT + (row + 1) * size, 0:128] = row_operand(shard, scales).astype(BF16)
        row_v[:, row * size : (row + 1) * size] = shard[COORDS:].astype(BF16)
    for hop in range(HOPS + 1):
        shard = own_ref[...] if hop == 0 else cols_ref[hop - 1]
        col_x[:, hop * size : (hop + 1) * size] = col_operand(shard, scales)
        col_v[:, hop * size : (hop + 1) * size] = shard[COORDS:].astype(BF16)
    acc_r[...] = jnp.zeros_like(acc_r)
    acc_c[...] = jnp.zeros_like(acc_c)
    upper = (lax.axis_index("tile") >= lax.axis_size("tile") // 2).astype(jnp.int32)

    def where(unit):
        shard, item = unit // PER_ROW, lax.rem(unit, PER_ROW)
        inner = item - 3
        row = jnp.where(item < 3, (item == 1).astype(jnp.int32), lax.rem(inner // 2, 2))
        row = jnp.where(item == 15, upper, jnp.where(item == 16, 1, row))
        col = jnp.where(item < 3, (item > 0).astype(jnp.int32), 2 * (1 + inner // 4) + lax.rem(inner, 2))
        col = jnp.where(item == 15, 8, jnp.where(item == 16, 8 + upper, col))
        one_way = (item < 2).astype(F32)
        return pl.multiple_of((shard * halves + row) * UNIT, UNIT), pl.multiple_of(col * UNIT, UNIT), 1.0 - one_way

    chunk = 256

    def distances(row, col, at):
        rows = work[pl.ds(pl.multiple_of(2 * UNIT + row + at, chunk), chunk), 0:DEPTH]
        return jnp.dot(rows, col_x[:, pl.ds(col, UNIT)], preferred_element_type=F32)

    def products(base, row, col, both, at):
        part = work[pl.ds(pl.multiple_of(base + at, chunk), chunk), :]
        rows = pl.ds(pl.multiple_of(row + at, chunk), chunk)
        cols = pl.ds(col, UNIT)
        acc_c[:, cols] += jnp.dot(row_v[:, rows], part, preferred_element_type=F32)
        acc_r[:, rows] += both * lax.dot_general(
            col_v[:, cols], part, (((1,), (1,)), ((), ())), preferred_element_type=F32
        )

    def step(unit, carry):
        base = pl.multiple_of(lax.rem(unit, 2) * UNIT, UNIT)
        last = pl.multiple_of(UNIT - base, UNIT)
        next_row, next_col, _ = where(jnp.minimum(unit + 1, units - 1))
        last_row, last_col, both = where(jnp.maximum(unit - 1, 0))
        for at in range(0, UNIT, chunk):
            fresh = distances(next_row, next_col, at)
            products(last, last_row, last_col, both, at)
            for line in range(at, at + chunk, 16):
                work[pl.ds(pl.multiple_of(base + line, 16), 16), :] = matern(small[line : line + 16, :])
            small[at : at + chunk, :] = fresh
        return carry

    first_row, first_col, _ = where(0)
    work[0 : 2 * UNIT, :] = jnp.zeros((2 * UNIT, UNIT), BF16)
    for at in range(0, UNIT, chunk):
        small[at : at + chunk, :] = distances(first_row, first_col, at)
    lax.fori_loop(0, units, step, 0)
    last_row, last_col, both = where(units - 1)
    for at in range(0, UNIT, chunk):
        products(((units - 1) % 2) * UNIT, last_row, last_col, both, at)
    for row in range(3):
        rows_out[row] = acc_r[:, row * size : (row + 1) * size]
    for hop in range(HOPS + 1):
        cols_out[hop] = acc_c[:, hop * size : (hop + 1) * size]


def vmem(count):
    return [pl.BlockSpec(memory_space=VMEM)] * count


def local(points, scales, vectors, plan):
    size = points.shape[1]
    own = jnp.concatenate([points, vectors], 0)
    stack = own.shape[0]
    smem = [pl.BlockSpec(memory_space=pltpu.SMEM)]
    shard = jax.ShapeDtypeStruct((stack, size), F32)
    dma = pltpu.SemaphoreType.DMA
    cols, far, near = pl.pallas_call(
        fetch_kernel,
        out_shape=(jax.ShapeDtypeStruct((HOPS, stack, size), F32), shard, shard),
        in_specs=smem + vmem(1),
        out_specs=vmem(3),
        scratch_shapes=[VMEM((3, stack, size), F32), VMEM((4, stack, size), F32), dma((9,)), dma((9,))],
        compiler_params=pltpu.CompilerParams(collective_id=0, has_side_effects=True),
    )(plan, own)
    row_sums, col_sums = pl.pallas_call(
        pair_kernel,
        out_shape=(
            jax.ShapeDtypeStruct((3, RHS, size), F32),
            jax.ShapeDtypeStruct((HOPS + 1, RHS, size), F32),
        ),
        in_specs=vmem(5),
        out_specs=vmem(2),
        scratch_shapes=[
            VMEM((UNIT, UNIT), F32),
            VMEM((2 * UNIT + 3 * size, UNIT), BF16),
            VMEM((DEPTH, (HOPS + 1) * size), BF16),
            VMEM((RHS, (HOPS + 1) * size), BF16),
            VMEM((RHS, 3 * size), BF16),
            VMEM((RHS, 3 * size), F32),
            VMEM((RHS, (HOPS + 1) * size), F32),
        ],
        compiler_params=pltpu.CompilerParams(vmem_limit_bytes=40 << 20),
    )(scales[:, None], own, cols, far, near)
    return pl.pallas_call(
        give_kernel,
        out_shape=jax.ShapeDtypeStruct((RHS, size), F32),
        in_specs=smem + vmem(3),
        out_specs=vmem(1)[0],
        scratch_shapes=[
            VMEM((HOPS, RHS, size), F32),
            VMEM((RHS, size), F32),
            VMEM((3, RHS, size), F32),
            VMEM((4, RHS, size), F32),
            dma((9,)),
            dma((9,)),
        ],
        compiler_params=pltpu.CompilerParams(collective_id=1, has_side_effects=True),
    )(plan, vectors, row_sums, col_sums)


def solution(mesh):
    placed = (P(None, ("team", "tile")), P(), P(None, ("team", "tile")), P())
    return jax.shard_map(
        local, mesh=mesh, in_specs=placed, out_specs=P(None, ("team", "tile")), check_vma=False
    )
```

```python
import functools
import math

import jax
import jax.numpy as jnp
from jax import lax
from jax.experimental import pallas as pl
from jax.experimental.pallas import tpu as pltpu
from jax.sharding import PartitionSpec as P

MESH = pl.DeviceIdType.MESH
VMEM = pltpu.VMEM
F32 = jnp.float32
BF16 = jnp.bfloat16

SHRINK = math.sqrt(0.05)
RATE = -10.0 / math.log(2.0)
COORDS = 8
RHS = 16
DEPTH = 64
UNIT = 512
HOPS = 4
PER_ROW = 17


def tile_id(offset):
    count = lax.axis_size("tile")
    return {"tile": lax.rem(lax.axis_index("tile") + offset + count, count)}


def team_id(pairing):
    me = lax.axis_index("team")
    bits = lax.axis_size("team").bit_length() - 1
    other = me * 0
    for bit in range(bits):
        mine = lax.rem(me // (1 << bit), 2)
        other = other + (1 << bit) * (1 - mine if pairing >> bit & 1 else mine)
    return {"team": other}


def greet(friends):
    barrier = pltpu.get_barrier_semaphore()
    for friend in friends:
        pl.semaphore_signal(barrier, inc=1, device_id=friend, device_id_type=MESH)
    pl.semaphore_wait(barrier, len(friends))


def remote(src, dst, send, recv, target):
    return pltpu.make_async_remote_copy(
        src_ref=src, dst_ref=dst, send_sem=send, recv_sem=recv, device_id=target, device_id_type=MESH
    )


def pieces(value, count):
    out = []
    for _ in range(count):
        piece = value.astype(BF16).astype(F32)
        out.append(piece)
        value = value - piece
    return out


def split(shard, scales):
    scaled = shard[:COORDS] / scales * SHRINK
    one, two, three = pieces(scaled, 3)
    norm = jnp.sum(scaled * scaled, axis=0, keepdims=True)
    return one, two, three, pieces(norm, 3)


def place(parts, size):
    row = lax.broadcasted_iota(jnp.int32, (8, size), 0)
    out = jnp.zeros((8, size), F32)
    for at, part in enumerate(parts):
        out = jnp.where(row == at, part, out)
    return out


def col_operand(shard, scales):
    one, two, three, norms = split(shard, scales)
    unit = jnp.ones_like(norms[0])
    tail = place(norms + [unit] * 3, shard.shape[1])
    return jnp.concatenate([one, one, one, two, two, three, tail, jnp.zeros_like(tail)], 0).astype(BF16)


def row_operand(shard, scales):
    one, two, three, norms = split(shard, scales)
    unit = jnp.ones_like(norms[0])
    tail = place([unit] * 3 + norms, shard.shape[1])
    stack = [-2.0 * one, -2.0 * two, -2.0 * three, -2.0 * one, -2.0 * two, -2.0 * one, tail]
    stack += [jnp.zeros_like(tail)] * 9
    return jnp.concatenate(stack, 0).T


def matern(small):
    small = jnp.maximum(small, 1e-30)
    w = small * lax.rsqrt(small)
    return ((w * (w + 0.3) + 0.03) * jnp.exp2(w * RATE)).astype(BF16)


def kernel(
    pairing,
    scales_ref,
    points_ref,
    vectors_ref,
    out_ref,
    own,
    came,
    small,
    work,
    col_x,
    col_v,
    row_v,
    acc_r,
    acc_c,
    back,
    sends,
    recvs,
):
    size = points_ref.shape[1]
    halves = size // UNIT
    units = 3 * PER_ROW
    far_team, near_team = team_id(15), team_id(pairing)
    own[0:COORDS, :] = points_ref[...]
    own[COORDS : COORDS + RHS, :] = vectors_ref[...]
    greet([tile_id(step) for step in range(1, lax.axis_size("tile"))] + [far_team, near_team])

    def fetch(slot):
        target = tile_id(-1 - slot) if slot < HOPS else (far_team if slot == HOPS else near_team)
        return remote(own, came.at[slot], sends.at[slot], recvs.at[slot], target)

    def give(slot):
        target = tile_id(1 + slot) if slot < HOPS else (far_team if slot == HOPS else near_team)
        if slot < HOPS:
            src = acc_c.at[:, (slot + 1) * size : (slot + 2) * size]
        else:
            src = acc_r.at[:, (slot - 3) * size : (slot - 2) * size]
        return remote(src, back.at[slot], sends.at[6 + slot], recvs.at[6 + slot], target)

    for slot in (0, 4, 1, 2, 3, 5):
        fetch(slot).start()

    line = lax.broadcasted_iota(jnp.int32, (COORDS, 1), 0)
    scales = jnp.zeros((COORDS, 1), F32)
    for coord in range(COORDS):
        scales = jnp.where(line == coord, scales_ref[coord], scales)

    def ready_row(shard, row):
        work[2 * UNIT + row * size : 2 * UNIT + (row + 1) * size, 0:128] = row_operand(shard, scales).astype(BF16)
        row_v[:, row * size : (row + 1) * size] = shard[COORDS:].astype(BF16)

    def ready_col(shard, hop):
        col_x[:, hop * size : (hop + 1) * size] = col_operand(shard, scales)
        col_v[:, hop * size : (hop + 1) * size] = shard[COORDS:].astype(BF16)

    ready_row(own[...], 0)
    ready_col(own[...], 0)
    acc_r[...] = jnp.zeros_like(acc_r)
    acc_c[...] = jnp.zeros_like(acc_c)
    upper = (lax.axis_index("tile") >= lax.axis_size("tile") // 2).astype(jnp.int32)

    def where(unit):
        shard = jnp.where(unit < 7, 0, jnp.where(unit < 24, 1, jnp.where(unit < 41, 2, 0)))
        item = jnp.where(unit < 7, unit, jnp.where(unit < 24, unit - 7, unit - 24))
        item = jnp.where(unit < 41, item, jnp.where(unit < 43, unit - 26, jnp.where(unit < 47, unit - 32, unit - 40)))
        inner = item - 3
        row = jnp.where(item < 3, (item == 1).astype(jnp.int32), lax.rem(inner // 2, 2))
        row = jnp.where(item == 15, upper, jnp.where(item == 16, 1, row))
        col = jnp.where(item < 3, (item > 0).astype(jnp.int32), 2 * (1 + inner // 4) + lax.rem(inner, 2))
        col = jnp.where(item == 15, 8, jnp.where(item == 16, 8 + upper, col))
        one_way = (item < 2).astype(F32)
        return pl.multiple_of((shard * halves + row) * UNIT, UNIT), pl.multiple_of(col * UNIT, UNIT), 1.0 - one_way

    chunk = 256

    def distances(row, col, at):
        rows = work[pl.ds(pl.multiple_of(2 * UNIT + row + at, chunk), chunk), 0:DEPTH]
        return jnp.dot(rows, col_x[:, pl.ds(col, UNIT)], preferred_element_type=F32)

    def products(base, row, col, both, at):
        part = work[pl.ds(pl.multiple_of(base + at, chunk), chunk), :]
        rows = pl.ds(pl.multiple_of(row + at, chunk), chunk)
        cols = pl.ds(col, UNIT)
        acc_c[:, cols] += jnp.dot(row_v[:, rows], part, preferred_element_type=F32)
        acc_r[:, rows] += both * lax.dot_general(
            col_v[:, cols], part, (((1,), (1,)), ((), ())), preferred_element_type=F32
        )

    def step(unit, carry):
        for start, slot in ((3, 0), (7, 4), (14, 1), (18, 2), (22, 3), (24, 5)):

            @pl.when(unit == start - 1)
            def _(slot=slot):
                fetch(slot).wait_recv()
                if slot < HOPS:
                    ready_col(came[slot], slot + 1)
                else:
                    ready_row(came[slot], slot - 3)

        for after, slots in ((25, (4,)), (42, (5, 0)), (44, (3,)), (48, (2,))):

            @pl.when(unit == after)
            def _(slots=slots):
                for slot in slots:
                    give(slot).start()

        base = pl.multiple_of(lax.rem(unit, 2) * UNIT, UNIT)
        last = pl.multiple_of(UNIT - base, UNIT)
        next_row, next_col, _ = where(jnp.minimum(unit + 1, units - 1))
        last_row, last_col, both = where(jnp.maximum(unit - 1, 0))
        for at in range(0, UNIT, chunk):
            fresh = distances(next_row, next_col, at)
            products(last, last_row, last_col, both, at)
            for line in range(at, at + chunk, 16):
                work[pl.ds(pl.multiple_of(base + line, 16), 16), :] = matern(small[line : line + 16, :])
            small[at : at + chunk, :] = fresh
        return carry

    first_row, first_col, _ = where(0)
    work[0 : 2 * UNIT, :] = jnp.zeros((2 * UNIT, UNIT), BF16)
    for at in range(0, UNIT, chunk):
        small[at : at + chunk, :] = distances(first_row, first_col, at)
    lax.fori_loop(0, units, step, 0)
    last_row, last_col, both = where(units - 1)
    for at in range(0, UNIT, chunk):
        products(((units - 1) % 2) * UNIT, last_row, last_col, both, at)
    give(1).start()
    total = 0.5 * vectors_ref[...] + acc_r[:, 0:size] + acc_c[:, 0:size]
    for slot in (4, 5, 0, 3, 2, 1):
        give(slot).wait_recv()
        total = total + back[slot]
    out_ref[...] = total
    for slot in range(6):
        fetch(slot).wait_send()
        give(slot).wait_send()


def vmem(count):
    return [pl.BlockSpec(memory_space=VMEM)] * count


def paired(pairing):
    def call(scales, points, vectors):
        size = points.shape[1]
        dma = pltpu.SemaphoreType.DMA
        return pl.pallas_call(
            functools.partial(kernel, pairing),
            out_shape=jax.ShapeDtypeStruct((RHS, size), F32),
            in_specs=[pl.BlockSpec(memory_space=pltpu.SMEM)] + vmem(2),
            out_specs=vmem(1)[0],
            scratch_shapes=[
                VMEM((COORDS + RHS, size), F32),
                VMEM((6, COORDS + RHS, size), F32),
                VMEM((UNIT, UNIT), F32),
                VMEM((2 * UNIT + 3 * size, UNIT), BF16),
                VMEM((DEPTH, (HOPS + 1) * size), BF16),
                VMEM((RHS, (HOPS + 1) * size), BF16),
                VMEM((RHS, 3 * size), BF16),
                VMEM((RHS, 3 * size), F32),
                VMEM((RHS, (HOPS + 1) * size), F32),
                VMEM((6, RHS, size), F32),
                dma((12,)),
                dma((12,)),
            ],
            compiler_params=pltpu.CompilerParams(
                collective_id=pairing - 1, has_side_effects=True, vmem_limit_bytes=40 << 20
            ),
        )(scales, points, vectors)

    return call


def local(points, scales, vectors, plan):
    pairing = plan[0] + plan[1] - 15
    return lax.switch(pairing - 1, [paired(number) for number in range(1, 15)], scales, points, vectors)


def solution(mesh):
    placed = (P(None, ("team", "tile")), P(), P(None, ("team", "tile")), P())
    return jax.shard_map(
        local, mesh=mesh, in_specs=placed, out_specs=P(None, ("team", "tile")), check_vma=False
    )
```

```python
import functools
import math

import jax
import jax.numpy as jnp
from jax import lax
from jax.experimental import pallas as pl
from jax.experimental.pallas import tpu as pltpu
from jax.sharding import PartitionSpec as P

MESH = pl.DeviceIdType.MESH
VMEM = pltpu.VMEM
F32 = jnp.float32
BF16 = jnp.bfloat16

SHRINK = math.sqrt(0.05)
RATE = -10.0 / math.log(2.0)
COORDS = 8
RHS = 16
DEPTH = 64
UNIT = 512
CHUNK = 256
HOPS = 4
HOME = 17
AWAY = 16


def tile_id(offset):
    count = lax.axis_size("tile")
    return {"tile": lax.rem(lax.axis_index("tile") + offset + count, count)}


def team_id(pairing):
    me = lax.axis_index("team")
    bits = lax.axis_size("team").bit_length() - 1
    other = me * 0
    for bit in range(bits):
        mine = lax.rem(me // (1 << bit), 2)
        other = other + (1 << bit) * (1 - mine if pairing >> bit & 1 else mine)
    return {"team": other}


def greet(friends):
    barrier = pltpu.get_barrier_semaphore()
    for friend in friends:
        pl.semaphore_signal(barrier, inc=1, device_id=friend, device_id_type=MESH)
    pl.semaphore_wait(barrier, len(friends))


def remote(src, dst, send, recv, target):
    return pltpu.make_async_remote_copy(
        src_ref=src, dst_ref=dst, send_sem=send, recv_sem=recv, device_id=target, device_id_type=MESH
    )


def pieces(value, count):
    out = []
    for _ in range(count):
        piece = value.astype(BF16).astype(F32)
        out.append(piece)
        value = value - piece
    return out


def split(shard, scales):
    scaled = shard[:COORDS] / scales * SHRINK
    one, two, three = pieces(scaled, 3)
    norm = jnp.sum(scaled * scaled, axis=0, keepdims=True)
    return one, two, three, pieces(norm, 3)


def place(parts, size):
    row = lax.broadcasted_iota(jnp.int32, (8, size), 0)
    out = jnp.zeros((8, size), F32)
    for at, part in enumerate(parts):
        out = jnp.where(row == at, part, out)
    return out


def col_operand(shard, scales):
    one, two, three, norms = split(shard, scales)
    unit = jnp.ones_like(norms[0])
    tail = place(norms + [unit] * 3, shard.shape[1])
    return jnp.concatenate([one, one, one, two, two, three, tail, jnp.zeros_like(tail)], 0).astype(BF16)


def row_operand(shard, scales):
    one, two, three, norms = split(shard, scales)
    unit = jnp.ones_like(norms[0])
    tail = place([unit] * 3 + norms, shard.shape[1])
    stack = [-2.0 * one, -2.0 * two, -2.0 * three, -2.0 * one, -2.0 * two, -2.0 * one, tail]
    stack += [jnp.zeros_like(tail)] * 9
    return jnp.concatenate(stack, 0).T


def matern(small):
    small = jnp.maximum(small, 1e-30)
    w = small * lax.rsqrt(small)
    return ((w * (w + 0.3) + 0.03) * jnp.exp2(w * RATE)).astype(BF16)


def kernel(
    pairing,
    scales_ref,
    points_ref,
    vectors_ref,
    out_ref,
    own,
    came,
    small,
    held,
    row_x,
    col_x,
    col_v,
    row_v,
    acc_r,
    acc_c,
    back,
    sends,
    recvs,
):
    size = points_ref.shape[1]
    halves = size // UNIT
    units = HOME + 2 * AWAY
    far_team, near_team = team_id(15), team_id(pairing)
    me = lax.axis_index("team")
    own[0:COORDS, :] = points_ref[...]
    own[COORDS : COORDS + RHS, :] = vectors_ref[...]
    greet([tile_id(step) for step in range(1, lax.axis_size("tile"))] + [far_team, near_team])

    def fetch(slot):
        target = tile_id(-1 - slot) if slot < HOPS else (far_team if slot == HOPS else near_team)
        return remote(own, came.at[slot], sends.at[slot], recvs.at[slot], target)

    def give(slot):
        target = tile_id(1 + slot) if slot < HOPS else (far_team if slot == HOPS else near_team)
        if slot < HOPS:
            src = acc_c.at[:, (slot + 1) * size : (slot + 2) * size]
        else:
            src = acc_r.at[:, (slot - 3) * size : (slot - 2) * size]
        return remote(src, back.at[slot], sends.at[6 + slot], recvs.at[6 + slot], target)

    for slot in (0, 4, 1, 2, 3, 5):
        fetch(slot).start()

    line = lax.broadcasted_iota(jnp.int32, (COORDS, 1), 0)
    scales = jnp.zeros((COORDS, 1), F32)
    for coord in range(COORDS):
        scales = jnp.where(line == coord, scales_ref[coord], scales)

    def ready_row(shard, row):
        row_x[row * size : (row + 1) * size, :] = row_operand(shard, scales).astype(BF16)
        row_v[:, row * size : (row + 1) * size] = shard[COORDS:].astype(BF16)

    def ready_col(shard, hop):
        col_x[:, hop * size : (hop + 1) * size] = col_operand(shard, scales)
        col_v[:, hop * size : (hop + 1) * size] = shard[COORDS:].astype(BF16)

    ready_row(own[...], 0)
    ready_col(own[...], 0)
    acc_r[...] = jnp.zeros_like(acc_r)
    acc_c[...] = jnp.zeros_like(acc_c)
    upper = (lax.axis_index("tile") >= lax.axis_size("tile") // 2).astype(jnp.int32)
    far_shift = (me > far_team["team"]).astype(jnp.int32)
    near_shift = (me > near_team["team"]).astype(jnp.int32)

    def where(unit):
        far, near = unit >= 7, unit >= 7 + AWAY
        late = unit >= 7 + 2 * AWAY
        shard = jnp.where(late, 0, near.astype(jnp.int32) + far.astype(jnp.int32))
        index = jnp.where(far, jnp.where(near, unit - 7 - AWAY, unit - 7), unit - 3)
        place = jnp.where(far, jnp.where(near, near_shift, far_shift), 1)
        index = jnp.where(late, jnp.where(unit < 45, unit - 41, unit - 45), index)
        place = jnp.where(late, jnp.where(unit < 45, 3, 2), place)
        row = lax.rem(index // 2, 2)
        col = 2 * (place + index // 4) + lax.rem(index, 2)
        row = jnp.where(unit < 3, (unit == 1).astype(jnp.int32), row)
        col = jnp.where(unit < 3, (unit > 0).astype(jnp.int32), col)
        row = jnp.where(unit == 39, upper, jnp.where(unit == 40, 1, row))
        col = jnp.where(unit == 39, 8, jnp.where(unit == 40, 8 + upper, col))
        return (shard * halves + row) * UNIT, col * UNIT, (unit >= 2).astype(F32)

    def distances(row, col, at):
        rows = row_x[pl.ds(pl.multiple_of(row + at, CHUNK), CHUNK), 0:DEPTH]
        return jnp.dot(rows, col_x[:, pl.ds(pl.multiple_of(col, UNIT), UNIT)], preferred_element_type=F32)

    def products(row, col, both, at):
        part = held[at // CHUNK]
        rows = pl.ds(pl.multiple_of(row + at, CHUNK), CHUNK)
        cols = pl.ds(pl.multiple_of(col, UNIT), UNIT)
        acc_c[:, cols] += jnp.dot(row_v[:, rows], part, preferred_element_type=F32)
        acc_r[:, rows] += both * lax.dot_general(
            col_v[:, cols], part, (((1,), (1,)), ((), ())), preferred_element_type=F32
        )

    def step(unit, carry):
        for start, slot in ((3, 0), (7, 4), (11, 1), (15, 2), (19, 3), (23, 5)):

            @pl.when(unit == start - 1)
            def _(slot=slot):
                fetch(slot).wait_recv()
                if slot < HOPS:
                    ready_col(came[slot], slot + 1)
                else:
                    ready_row(came[slot], slot - 3)

        for after, slots in ((24, (4,)), (32, (0,)), (40, (5,)), (42, (3,)), (46, (2,))):

            @pl.when(unit == after)
            def _(slots=slots):
                for slot in slots:
                    give(slot).start()

        last, current = carry
        following = where(jnp.minimum(unit + 1, units - 1))
        for at in range(0, UNIT, CHUNK):
            fresh = distances(following[0], following[1], at)
            if at == 0:
                products(*last, UNIT - CHUNK)
            else:
                products(*current, at - CHUNK)
            for line in range(0, CHUNK, 16):
                held[at // CHUNK, line : line + 16, :] = matern(small[at + line : at + line + 16, :])
            small[at : at + CHUNK, :] = fresh
        return current, following

    first = where(jnp.int32(0))
    held[...] = jnp.zeros_like(held)
    for at in range(0, UNIT, CHUNK):
        small[at : at + CHUNK, :] = distances(first[0], first[1], at)
    last, _ = lax.fori_loop(0, units, step, (first, first))
    products(*last, UNIT - CHUNK)
    give(1).start()
    total = 0.5 * vectors_ref[...] + acc_r[:, 0:size] + acc_c[:, 0:size]
    for slot in (4, 5, 0, 3, 2, 1):
        give(slot).wait_recv()
        total = total + back[slot]
    out_ref[...] = total
    for slot in range(6):
        fetch(slot).wait_send()
        give(slot).wait_send()


def vmem(count):
    return [pl.BlockSpec(memory_space=VMEM)] * count


def paired(pairing):
    def call(scales, points, vectors):
        size = points.shape[1]
        dma = pltpu.SemaphoreType.DMA
        return pl.pallas_call(
            functools.partial(kernel, pairing),
            out_shape=jax.ShapeDtypeStruct((RHS, size), F32),
            in_specs=[pl.BlockSpec(memory_space=pltpu.SMEM)] + vmem(2),
            out_specs=vmem(1)[0],
            scratch_shapes=[
                VMEM((COORDS + RHS, size), F32),
                VMEM((6, COORDS + RHS, size), F32),
                VMEM((UNIT, UNIT), F32),
                VMEM((UNIT // CHUNK, CHUNK, UNIT), BF16),
                VMEM((3 * size, 128), BF16),
                VMEM((DEPTH, (HOPS + 1) * size), BF16),
                VMEM((RHS, (HOPS + 1) * size), BF16),
                VMEM((RHS, 3 * size), BF16),
                VMEM((RHS, 3 * size), F32),
                VMEM((RHS, (HOPS + 1) * size), F32),
                VMEM((6, RHS, size), F32),
                dma((12,)),
                dma((12,)),
            ],
            compiler_params=pltpu.CompilerParams(
                collective_id=pairing - 1, has_side_effects=True, vmem_limit_bytes=40 << 20
            ),
        )(scales, points, vectors)

    return call


def local(points, scales, vectors, plan):
    pairing = plan[0] + plan[1] - 15
    return lax.switch(pairing - 1, [paired(number) for number in range(1, 15)], scales, points, vectors)


def solution(mesh):
    placed = (P(None, ("team", "tile")), P(), P(None, ("team", "tile")), P())
    return jax.shard_map(
        local, mesh=mesh, in_specs=placed, out_specs=P(None, ("team", "tile")), check_vma=False
    )
```

```python
import functools
import math

import jax
import jax.numpy as jnp
from jax import lax
from jax.experimental import pallas as pl
from jax.experimental.pallas import tpu as pltpu
from jax.sharding import PartitionSpec as P

MESH = pl.DeviceIdType.MESH
VMEM = pltpu.VMEM
F32 = jnp.float32
BF16 = jnp.bfloat16

SHRINK = math.sqrt(0.05)
RATE = -10.0 / math.log(2.0)
COORDS = 8
RHS = 16
DEPTH = 64
UNIT = 512
CHUNK = 256
HOPS = 4
ORDER = ((0, 0), (0, 1), (2, 0), (2, 1), (2, 2), (2, 3), (0, 3), (0, 4), (1, 3), (1, 2), (1, 1), (1, 0), (0, 2))
SENDS = {1: -1, 5: -1, 0: -1, 2: -1, 3: -1, 4: -1}


def tile_id(offset):
    count = lax.axis_size("tile")
    return {"tile": lax.rem(lax.axis_index("tile") + offset + count, count)}


def team_id(pairing):
    me = lax.axis_index("team")
    bits = lax.axis_size("team").bit_length() - 1
    other = me * 0
    for bit in range(bits):
        mine = lax.rem(me // (1 << bit), 2)
        other = other + (1 << bit) * (1 - mine if pairing >> bit & 1 else mine)
    return {"team": other}


def greet(friends):
    barrier = pltpu.get_barrier_semaphore()
    for friend in friends:
        pl.semaphore_signal(barrier, inc=1, device_id=friend, device_id_type=MESH)
    pl.semaphore_wait(barrier, len(friends))


def remote(src, dst, send, recv, target):
    return pltpu.make_async_remote_copy(
        src_ref=src, dst_ref=dst, send_sem=send, recv_sem=recv, device_id=target, device_id_type=MESH
    )


def pieces(value, count):
    out = []
    for _ in range(count):
        piece = value.astype(BF16).astype(F32)
        out.append(piece)
        value = value - piece
    return out


def split(shard, scales):
    scaled = shard[:COORDS] / scales * SHRINK
    one, two, three = pieces(scaled, 3)
    norm = jnp.sum(scaled * scaled, axis=0, keepdims=True)
    return one, two, three, pieces(norm, 3)


def place(parts, size):
    row = lax.broadcasted_iota(jnp.int32, (8, size), 0)
    out = jnp.zeros((8, size), F32)
    for at, part in enumerate(parts):
        out = jnp.where(row == at, part, out)
    return out


def col_operand(shard, scales):
    one, two, three, norms = split(shard, scales)
    unit = jnp.ones_like(norms[0])
    tail = place(norms + [unit] * 3, shard.shape[1])
    return jnp.concatenate([one, one, one, two, two, three, tail, jnp.zeros_like(tail)], 0).astype(BF16)


def row_operand(shard, scales):
    one, two, three, norms = split(shard, scales)
    unit = jnp.ones_like(norms[0])
    tail = place([unit] * 3 + norms, shard.shape[1])
    stack = [-2.0 * one, -2.0 * two, -2.0 * three, -2.0 * one, -2.0 * two, -2.0 * one, tail]
    stack += [jnp.zeros_like(tail)] * 9
    return jnp.concatenate(stack, 0).T


def matern(small):
    small = jnp.maximum(small, 1e-30)
    w = small * lax.rsqrt(small)
    return ((w * (w + 0.3) + 0.03) * jnp.exp2(w * RATE)).astype(BF16)


def kernel(
    pairing,
    scales_ref,
    points_ref,
    vectors_ref,
    out_ref,
    own,
    came,
    small,
    held,
    row_x,
    col_x,
    col_v,
    row_v,
    acc_r,
    acc_c,
    back,
    sends,
    recvs,
):
    size = points_ref.shape[1]
    halves = size // UNIT
    far_team, near_team = team_id(15), team_id(pairing)
    me = lax.axis_index("team")
    own[0:COORDS, :] = points_ref[...]
    own[COORDS : COORDS + RHS, :] = vectors_ref[...]
    greet([tile_id(step) for step in range(1, lax.axis_size("tile"))] + [far_team, near_team])

    def fetch(slot):
        target = tile_id(-1 - slot) if slot < HOPS else (far_team if slot == HOPS else near_team)
        return remote(own, came.at[slot], sends.at[slot], recvs.at[slot], target)

    def give(slot):
        target = tile_id(1 + slot) if slot < HOPS else (far_team if slot == HOPS else near_team)
        if slot < HOPS:
            src = acc_c.at[:, (slot + 1) * size : (slot + 2) * size]
        else:
            src = acc_r.at[:, (slot - 3) * size : (slot - 2) * size]
        return remote(src, back.at[slot], sends.at[6 + slot], recvs.at[6 + slot], target)

    for slot in SENDS:
        if SENDS[slot] < 0:
            fetch(slot).start()

    line = lax.broadcasted_iota(jnp.int32, (COORDS, 1), 0)
    scales = jnp.zeros((COORDS, 1), F32)
    for coord in range(COORDS):
        scales = jnp.where(line == coord, scales_ref[coord], scales)

    def ready_row(shard, row):
        row_x[row * size : (row + 1) * size, :] = row_operand(shard, scales).astype(BF16)
        row_v[:, row * size : (row + 1) * size] = shard[COORDS:].astype(BF16)

    def ready_col(shard, hop):
        col_x[:, hop * size : (hop + 1) * size] = col_operand(shard, scales)
        col_v[:, hop * size : (hop + 1) * size] = shard[COORDS:].astype(BF16)

    ready_row(own[...], 0)
    ready_col(own[...], 0)
    acc_r[...] = jnp.zeros_like(acc_r)
    acc_c[...] = jnp.zeros_like(acc_c)
    upper = (lax.axis_index("tile") >= lax.axis_size("tile") // 2).astype(jnp.int32)
    shifts = [jnp.int32(0)] + [(me > team["team"]).astype(jnp.int32) for team in (far_team, near_team)]
    counts = [3 if group == (0, 0) else 2 if group == (0, HOPS) else 4 for group in ORDER]
    starts = [sum(counts[:number]) for number in range(len(ORDER))]
    units = sum(counts)
    first_use, last_use = {}, {}
    for (shard, place), start, count in zip(ORDER, starts, counts):
        used = [place - 1] if shard == 0 else [place - 1, place, HOPS - 1 + shard]
        for slot in used:
            if slot >= 0:
                first_use.setdefault(slot, start)
                last_use[slot] = start + count - 1

    def where(unit):
        shard, place, index = jnp.int32(0), jnp.int32(0), unit
        for (group_shard, group_place), start in zip(ORDER[1:], starts[1:]):
            here = unit >= start
            shard = jnp.where(here, group_shard, shard)
            place = jnp.where(here, group_place + shifts[group_shard], place)
            index = jnp.where(here, unit - start, index)
        row = lax.rem(index // 2, 2)
        col = 2 * place + lax.rem(index, 2)
        row = jnp.where(unit < 3, (unit == 1).astype(jnp.int32), row)
        col = jnp.where(unit < 3, (unit > 0).astype(jnp.int32), col)
        half = starts[ORDER.index((0, HOPS))]
        row = jnp.where(unit == half, upper, jnp.where(unit == half + 1, 1, row))
        col = jnp.where(unit == half, 2 * HOPS, jnp.where(unit == half + 1, 2 * HOPS + upper, col))
        return (shard * halves + row) * UNIT, col * UNIT, (unit >= 2).astype(F32)

    def distances(row, col, at):
        rows = row_x[pl.ds(pl.multiple_of(row + at, CHUNK), CHUNK), 0:DEPTH]
        return jnp.dot(rows, col_x[:, pl.ds(pl.multiple_of(col, UNIT), UNIT)], preferred_element_type=F32)

    def products(row, col, both, at):
        part = held[at // CHUNK]
        rows = pl.ds(pl.multiple_of(row + at, CHUNK), CHUNK)
        cols = pl.ds(pl.multiple_of(col, UNIT), UNIT)
        acc_c[:, cols] += jnp.dot(row_v[:, rows], part, preferred_element_type=F32)
        acc_r[:, rows] += both * lax.dot_general(
            col_v[:, cols], part, (((1,), (1,)), ((), ())), preferred_element_type=F32
        )

    def step(unit, carry):
        for number in range(units):
            leaving = [slot for slot in SENDS if SENDS[slot] == number]
            coming = [slot for slot in first_use if first_use[slot] == number + 1]
            giving = [slot for slot in last_use if last_use[slot] == number - 2]
            if leaving or coming or giving:

                @pl.when(unit == number)
                def _(leaving=leaving, coming=coming, giving=giving):
                    for slot in leaving:
                        fetch(slot).start()
                    for slot in giving:
                        give(slot).start()
                    for slot in coming:
                        fetch(slot).wait_recv()
                        if slot < HOPS:
                            ready_col(came[slot], slot + 1)
                        else:
                            ready_row(came[slot], slot - 3)

        last, current, following = carry
        for at in range(0, UNIT, CHUNK):
            fresh = distances(following[0], following[1], at)
            if at == 0:
                products(*last, UNIT - CHUNK)
            else:
                products(*current, at - CHUNK)
            for line in range(0, CHUNK, 16):
                held[at // CHUNK, line : line + 16, :] = matern(small[at + line : at + line + 16, :])
            small[at : at + CHUNK, :] = fresh
        return current, following, where(jnp.minimum(unit + 2, units - 1))

    first = where(jnp.int32(0))
    held[...] = jnp.zeros_like(held)
    for at in range(0, UNIT, CHUNK):
        small[at : at + CHUNK, :] = distances(first[0], first[1], at)
    last, _, _ = lax.fori_loop(0, units, step, (first, first, where(jnp.int32(1))))
    products(*last, UNIT - CHUNK)
    for slot in last_use:
        if last_use[slot] > units - 3:
            give(slot).start()
    total = 0.5 * vectors_ref[...] + acc_r[:, 0:size] + acc_c[:, 0:size]
    for slot in sorted(last_use, key=lambda slot: last_use[slot]):
        give(slot).wait_recv()
        total = total + back[slot]
    out_ref[...] = total
    for slot in range(6):
        fetch(slot).wait_send()
        give(slot).wait_send()


def vmem(count):
    return [pl.BlockSpec(memory_space=VMEM)] * count


def paired(pairing):
    def call(scales, points, vectors):
        size = points.shape[1]
        dma = pltpu.SemaphoreType.DMA
        return pl.pallas_call(
            functools.partial(kernel, pairing),
            out_shape=jax.ShapeDtypeStruct((RHS, size), F32),
            in_specs=[pl.BlockSpec(memory_space=pltpu.SMEM)] + vmem(2),
            out_specs=vmem(1)[0],
            scratch_shapes=[
                VMEM((COORDS + RHS, size), F32),
                VMEM((6, COORDS + RHS, size), F32),
                VMEM((UNIT, UNIT), F32),
                VMEM((UNIT // CHUNK, CHUNK, UNIT), BF16),
                VMEM((3 * size, 128), BF16),
                VMEM((DEPTH, (HOPS + 1) * size), BF16),
                VMEM((RHS, (HOPS + 1) * size), BF16),
                VMEM((RHS, 3 * size), BF16),
                VMEM((RHS, 3 * size), F32),
                VMEM((RHS, (HOPS + 1) * size), F32),
                VMEM((6, RHS, size), F32),
                dma((12,)),
                dma((12,)),
            ],
            compiler_params=pltpu.CompilerParams(
                collective_id=pairing - 1, has_side_effects=True, vmem_limit_bytes=60 << 20
            ),
        )(scales, points, vectors)

    return call


def local(points, scales, vectors, plan):
    kernels = [paired(number) for number in range(1, 15)]
    return lax.switch(jnp.min(plan), [lambda scales, points, vectors: vectors] + kernels, scales, points, vectors)


def solution(mesh):
    placed = (P(None, ("team", "tile")), P(), P(None, ("team", "tile")), P())
    return jax.shard_map(
        local, mesh=mesh, in_specs=placed, out_specs=P(None, ("team", "tile")), check_vma=False
    )
```

```python
import functools
import math

import jax
import jax.numpy as jnp
from jax import lax
from jax.experimental import pallas as pl
from jax.experimental.pallas import tpu as pltpu
from jax.sharding import PartitionSpec as P

MESH = pl.DeviceIdType.MESH
VMEM = pltpu.VMEM
F32 = jnp.float32
BF16 = jnp.bfloat16

SHRINK = math.sqrt(0.05)
RATE = -10.0 / math.log(2.0)
COORDS = 8
RHS = 16
DEPTH = 64
UNIT = 512
CHUNK = 256
HOPS = 4
ORDER = ((0, 0), (0, 1), (2, 0), (2, 1), (2, 2), (2, 3), (0, 3), (0, 4), (1, 3), (1, 2), (1, 1), (1, 0), (0, 2))
SENDS = (1, 5, 0, 2, 3, 4)


def tile_id(offset):
    count = lax.axis_size("tile")
    return {"tile": lax.rem(lax.axis_index("tile") + offset + count, count)}


def team_id(pairing):
    me = lax.axis_index("team")
    bits = lax.axis_size("team").bit_length() - 1
    other = me * 0
    for bit in range(bits):
        mine = lax.rem(me // (1 << bit), 2)
        other = other + (1 << bit) * (1 - mine if pairing >> bit & 1 else mine)
    return {"team": other}


def greet(friends):
    barrier = pltpu.get_barrier_semaphore()
    for friend in friends:
        pl.semaphore_signal(barrier, inc=1, device_id=friend, device_id_type=MESH)
    pl.semaphore_wait(barrier, len(friends))


def remote(src, dst, send, recv, target):
    return pltpu.make_async_remote_copy(
        src_ref=src, dst_ref=dst, send_sem=send, recv_sem=recv, device_id=target, device_id_type=MESH
    )


def pieces(value, count):
    out = []
    for _ in range(count):
        piece = value.astype(BF16).astype(F32)
        out.append(piece)
        value = value - piece
    return out


def split(shard, scales):
    scaled = shard[:COORDS] / scales * SHRINK
    one, two, three = pieces(scaled, 3)
    norm = jnp.sum(scaled * scaled, axis=0, keepdims=True)
    return one, two, three, pieces(norm, 3)


def place(parts, size):
    row = lax.broadcasted_iota(jnp.int32, (8, size), 0)
    out = jnp.zeros((8, size), F32)
    for at, part in enumerate(parts):
        out = jnp.where(row == at, part, out)
    return out


def col_operand(shard, scales):
    one, two, three, norms = split(shard, scales)
    unit = jnp.ones_like(norms[0])
    tail = place(norms + [unit] * 3, shard.shape[1])
    return jnp.concatenate([one, one, one, two, two, three, tail, jnp.zeros_like(tail)], 0).astype(BF16)


def row_operand(shard, scales):
    one, two, three, norms = split(shard, scales)
    unit = jnp.ones_like(norms[0])
    tail = place([unit] * 3 + norms, shard.shape[1])
    stack = [-2.0 * one, -2.0 * two, -2.0 * three, -2.0 * one, -2.0 * two, -2.0 * one, tail]
    stack += [jnp.zeros_like(tail)] * 9
    return jnp.concatenate(stack, 0).T


def matern(small):
    small = jnp.maximum(small, 1e-30)
    w = small * lax.rsqrt(small)
    return ((w * (w + 0.3) + 0.03) * jnp.exp2(w * RATE)).astype(BF16)


def kernel(
    pairing,
    scales_ref,
    points_ref,
    vectors_ref,
    out_ref,
    own,
    came,
    small,
    held,
    row_x,
    col_x,
    col_v,
    row_v,
    acc_r,
    acc_c,
    back,
    sends,
    recvs,
    locals_sem,
):
    size = own.shape[1]
    halves = size // UNIT
    far_team, near_team = team_id(15), team_id(pairing)
    me = lax.axis_index("team")
    loads = [
        pltpu.make_async_copy(points_ref, own.at[0:COORDS], locals_sem.at[0]),
        pltpu.make_async_copy(vectors_ref, own.at[COORDS : COORDS + RHS], locals_sem.at[1]),
    ]
    for load in loads:
        load.start()
    greet([tile_id(step) for step in range(1, lax.axis_size("tile"))] + [far_team, near_team])

    for load in loads:
        load.wait()

    def fetch(slot):
        target = tile_id(-1 - slot) if slot < HOPS else (far_team if slot == HOPS else near_team)
        return remote(own, came.at[slot], sends.at[slot], recvs.at[slot], target)

    def give(slot):
        target = tile_id(1 + slot) if slot < HOPS else (far_team if slot == HOPS else near_team)
        if slot < HOPS:
            src = acc_c.at[:, (slot + 1) * size : (slot + 2) * size]
        else:
            src = acc_r.at[:, (slot - 3) * size : (slot - 2) * size]
        return remote(src, back.at[slot], sends.at[6 + slot], recvs.at[6 + slot], target)

    for slot in SENDS:
        fetch(slot).start()

    line = lax.broadcasted_iota(jnp.int32, (COORDS, 1), 0)
    scales = jnp.zeros((COORDS, 1), F32)
    for coord in range(COORDS):
        scales = jnp.where(line == coord, scales_ref[coord], scales)

    def ready_row(shard, row):
        at = pl.ds(pl.multiple_of(row * size, size), size)
        row_x[at, :] = row_operand(shard, scales).astype(BF16)
        row_v[:, at] = shard[COORDS:].astype(BF16)

    def ready_col(shard, hop):
        at = pl.ds(pl.multiple_of(hop * size, size), size)
        col_x[:, at] = col_operand(shard, scales)
        col_v[:, at] = shard[COORDS:].astype(BF16)

    ready_row(own[...], jnp.int32(0))
    ready_col(own[...], jnp.int32(0))
    acc_r[...] = jnp.zeros_like(acc_r)
    acc_c[...] = jnp.zeros_like(acc_c)
    upper = (lax.axis_index("tile") >= lax.axis_size("tile") // 2).astype(jnp.int32)
    shifts = [jnp.int32(0)] + [(me > team["team"]).astype(jnp.int32) for team in (far_team, near_team)]
    counts = [3 if group == (0, 0) else 2 if group == (0, HOPS) else 4 for group in ORDER]
    starts = [sum(counts[:number]) for number in range(len(ORDER))]
    units = sum(counts)
    first_use, last_use = {}, {}
    for (shard, place), start, count in zip(ORDER, starts, counts):
        used = [place - 1] if shard == 0 else [place - 1, place, HOPS - 1 + shard]
        for slot in used:
            if slot >= 0:
                first_use.setdefault(slot, start)
                last_use[slot] = start + count - 1

    for kind in (range(HOPS), range(HOPS, HOPS + 2)):
        taken = set()
        for slot in sorted(kind, key=lambda slot: -first_use[slot]):
            while first_use[slot] in taken:
                first_use[slot] -= 1
            taken.add(first_use[slot])

    def where(unit):
        shard, place, index = jnp.int32(0), jnp.int32(0), unit
        for (group_shard, group_place), start in zip(ORDER[1:], starts[1:]):
            here = unit >= start
            shard = jnp.where(here, group_shard, shard)
            place = jnp.where(here, group_place + shifts[group_shard], place)
            index = jnp.where(here, unit - start, index)
        row = lax.rem(index // 2, 2)
        col = 2 * place + lax.rem(index, 2)
        row = jnp.where(unit < 3, (unit == 1).astype(jnp.int32), row)
        col = jnp.where(unit < 3, (unit > 0).astype(jnp.int32), col)
        half = starts[ORDER.index((0, HOPS))]
        row = jnp.where(unit == half, upper, jnp.where(unit == half + 1, 1, row))
        col = jnp.where(unit == half, 2 * HOPS, jnp.where(unit == half + 1, 2 * HOPS + upper, col))
        return (shard * halves + row) * UNIT, col * UNIT, (unit >= 2).astype(F32)

    def distances(row, col, at):
        rows = row_x[pl.ds(pl.multiple_of(row + at, CHUNK), CHUNK), 0:DEPTH]
        return jnp.dot(rows, col_x[:, pl.ds(pl.multiple_of(col, UNIT), UNIT)], preferred_element_type=F32)

    def products(row, col, both, at):
        part = held[at // CHUNK]
        rows = pl.ds(pl.multiple_of(row + at, CHUNK), CHUNK)
        cols = pl.ds(pl.multiple_of(col, UNIT), UNIT)
        acc_c[:, cols] += jnp.dot(row_v[:, rows], part, preferred_element_type=F32)
        acc_r[:, rows] += both * lax.dot_general(
            col_v[:, cols], part, (((1,), (1,)), ((), ())), preferred_element_type=F32
        )

    def step(unit, carry):
        for number in range(units):
            giving = [slot for slot in last_use if last_use[slot] == number - 2]
            if giving:

                @pl.when(unit == number)
                def _(giving=giving):
                    for slot in giving:
                        give(slot).start()

        for slots, ready in ((range(HOPS), ready_col), (range(HOPS, HOPS + 2), ready_row)):
            due = [(slot, first_use[slot] - 1) for slot in slots]

            @pl.when(functools.reduce(jnp.logical_or, [unit == number for _, number in due]))
            def _(due=due, ready=ready, shift=1 if ready is ready_col else 1 - HOPS):
                slot = sum(jnp.where(unit == number, slot, 0) for slot, number in due)
                remote(own, came.at[slot], sends.at[slot], recvs.at[slot], far_team).wait_recv()
                ready(came[slot], slot + shift)

        last, current, following = carry
        for at in range(0, UNIT, CHUNK):
            fresh = distances(following[0], following[1], at)
            if at == 0:
                products(*last, UNIT - CHUNK)
            else:
                products(*current, at - CHUNK)
            for line in range(0, CHUNK, 16):
                held[at // CHUNK, line : line + 16, :] = matern(small[at + line : at + line + 16, :])
            small[at : at + CHUNK, :] = fresh
        return current, following, where(jnp.minimum(unit + 2, units - 1))

    first = where(jnp.int32(0))
    held[...] = jnp.zeros_like(held)
    for at in range(0, UNIT, CHUNK):
        small[at : at + CHUNK, :] = distances(first[0], first[1], at)
    last, _, _ = lax.fori_loop(0, units, step, (first, first, where(jnp.int32(1))))
    products(*last, UNIT - CHUNK)
    for slot in last_use:
        if last_use[slot] > units - 3:
            give(slot).start()
    total = 0.5 * own[COORDS : COORDS + RHS, :] + acc_r[:, 0:size] + acc_c[:, 0:size]
    for slot in sorted(last_use, key=lambda slot: last_use[slot]):
        give(slot).wait_recv()
        total = total + back[slot]
    out_ref[...] = total
    for slot in range(6):
        fetch(slot).wait_send()
        give(slot).wait_send()


def vmem(count):
    return [pl.BlockSpec(memory_space=VMEM)] * count


def paired(pairing):
    def call(scales, points, vectors):
        size = points.shape[1]
        dma = pltpu.SemaphoreType.DMA
        return pl.pallas_call(
            functools.partial(kernel, pairing),
            out_shape=jax.ShapeDtypeStruct((RHS, size), F32),
            in_specs=[pl.BlockSpec(memory_space=pltpu.SMEM)] + [pl.BlockSpec(memory_space=pl.ANY)] * 2,
            out_specs=vmem(1)[0],
            scratch_shapes=[
                VMEM((COORDS + RHS, size), F32),
                VMEM((6, COORDS + RHS, size), F32),
                VMEM((UNIT, UNIT), F32),
                VMEM((UNIT // CHUNK, CHUNK, UNIT), BF16),
                VMEM((3 * size, 128), BF16),
                VMEM((DEPTH, (HOPS + 1) * size), BF16),
                VMEM((RHS, (HOPS + 1) * size), BF16),
                VMEM((RHS, 3 * size), BF16),
                VMEM((RHS, 3 * size), F32),
                VMEM((RHS, (HOPS + 1) * size), F32),
                VMEM((6, RHS, size), F32),
                dma((12,)),
                dma((12,)),
                dma((2,)),
            ],
            compiler_params=pltpu.CompilerParams(
                collective_id=pairing - 1, has_side_effects=True, vmem_limit_bytes=60 << 20
            ),
        )(scales, points, vectors)

    return call


def local(points, scales, vectors, plan):
    kernels = [paired(number) for number in range(1, 15)]
    return lax.switch(jnp.min(plan), [lambda *args: jnp.zeros(vectors.shape, F32)] + kernels, scales, points, vectors)


def solution(mesh):
    placed = (P(None, ("team", "tile")), P(), P(None, ("team", "tile")), P())
    return jax.shard_map(
        local, mesh=mesh, in_specs=placed, out_specs=P(None, ("team", "tile")), check_vma=False
    )
```

```python
import functools
import math

import jax
import jax.numpy as jnp
from jax import lax
from jax.experimental import pallas as pl
from jax.experimental.pallas import tpu as pltpu
from jax.sharding import PartitionSpec as P

MESH = pl.DeviceIdType.MESH
VMEM = pltpu.VMEM
F32 = jnp.float32
BF16 = jnp.bfloat16

SHRINK = math.sqrt(0.05)
RATE = -10.0 / math.log(2.0)
COORDS = 8
RHS = 16
DEPTH = 64
UNIT = 512
CHUNK = 256
HOPS = 4
ORDER = ((0, 0), (0, 1), (2, 0), (2, 1), (2, 2), (2, 3), (0, 3), (0, 4), (1, 2), (1, 3), (1, 1), (1, 0), (0, 2))
SENDS = (0, 5, 1, 4, 2, 3)


def tile_id(offset):
    count = lax.axis_size("tile")
    return {"tile": lax.rem(lax.axis_index("tile") + offset + count, count)}


def team_id(pairing):
    me = lax.axis_index("team")
    bits = lax.axis_size("team").bit_length() - 1
    other = me * 0
    for bit in range(bits):
        mine = lax.rem(me // (1 << bit), 2)
        other = other + (1 << bit) * (1 - mine if pairing >> bit & 1 else mine)
    return {"team": other}


def greet(friends):
    barrier = pltpu.get_barrier_semaphore()
    for friend in friends:
        pl.semaphore_signal(barrier, inc=1, device_id=friend, device_id_type=MESH)
    pl.semaphore_wait(barrier, len(friends))


def remote(src, dst, send, recv, target):
    return pltpu.make_async_remote_copy(
        src_ref=src, dst_ref=dst, send_sem=send, recv_sem=recv, device_id=target, device_id_type=MESH
    )


def pieces(value, count):
    out = []
    for _ in range(count):
        piece = value.astype(BF16).astype(F32)
        out.append(piece)
        value = value - piece
    return out


def split(shard, scales):
    scaled = shard[:COORDS] / scales * SHRINK
    one, two, three = pieces(scaled, 3)
    norm = jnp.sum(scaled * scaled, axis=0, keepdims=True)
    return one, two, three, pieces(norm, 3)


def place(parts, size):
    row = lax.broadcasted_iota(jnp.int32, (8, size), 0)
    out = jnp.zeros((8, size), F32)
    for at, part in enumerate(parts):
        out = jnp.where(row == at, part, out)
    return out


def col_operand(shard, scales):
    one, two, three, norms = split(shard, scales)
    unit = jnp.ones_like(norms[0])
    tail = place(norms + [unit] * 3, shard.shape[1])
    return jnp.concatenate([one, one, one, two, two, three, tail, jnp.zeros_like(tail)], 0).astype(BF16)


def row_operand(shard, scales):
    one, two, three, norms = split(shard, scales)
    unit = jnp.ones_like(norms[0])
    tail = place([unit] * 3 + norms, shard.shape[1])
    stack = [-2.0 * one, -2.0 * two, -2.0 * three, -2.0 * one, -2.0 * two, -2.0 * one, tail]
    stack += [jnp.zeros_like(tail)] * 9
    return jnp.concatenate(stack, 0).T


def matern(small):
    small = jnp.maximum(small, 1e-30)
    w = small * lax.rsqrt(small)
    return ((w * (w + 0.3) + 0.03) * jnp.exp2(w * RATE)).astype(BF16)


def kernel(
    pairing,
    scales_ref,
    points_ref,
    vectors_ref,
    out_ref,
    own,
    came,
    small,
    held,
    row_x,
    col_x,
    col_v,
    row_v,
    acc_r,
    acc_c,
    back,
    sends,
    recvs,
    locals_sem,
):
    size = own.shape[1]
    halves = size // UNIT
    far_team, near_team = team_id(15), team_id(pairing)
    me = lax.axis_index("team")
    loads = [
        pltpu.make_async_copy(points_ref, own.at[0:COORDS], locals_sem.at[0]),
        pltpu.make_async_copy(vectors_ref, own.at[COORDS : COORDS + RHS], locals_sem.at[1]),
    ]
    for load in loads:
        load.start()
    greet([tile_id(step) for step in range(1, lax.axis_size("tile"))] + [far_team, near_team])

    for load in loads:
        load.wait()

    def fetch(slot):
        target = tile_id(-1 - slot) if slot < HOPS else (far_team if slot == HOPS else near_team)
        return remote(own, came.at[slot], sends.at[slot], recvs.at[slot], target)

    def give(slot):
        target = tile_id(1 + slot) if slot < HOPS else (far_team if slot == HOPS else near_team)
        if slot < HOPS:
            src = acc_c.at[:, (slot + 1) * size : (slot + 2) * size]
        else:
            src = acc_r.at[:, (slot - 3) * size : (slot - 2) * size]
        return remote(src, back.at[slot], sends.at[6 + slot], recvs.at[6 + slot], target)

    for slot in SENDS:
        fetch(slot).start()

    line = lax.broadcasted_iota(jnp.int32, (COORDS, 1), 0)
    scales = jnp.zeros((COORDS, 1), F32)
    for coord in range(COORDS):
        scales = jnp.where(line == coord, scales_ref[coord], scales)

    def ready_row(shard, row):
        at = pl.ds(pl.multiple_of(row * size, size), size)
        row_x[at, :] = row_operand(shard, scales).astype(BF16)
        row_v[:, at] = shard[COORDS:].astype(BF16)

    def ready_col(shard, hop):
        at = pl.ds(pl.multiple_of(hop * size, size), size)
        col_x[:, at] = col_operand(shard, scales)
        col_v[:, at] = shard[COORDS:].astype(BF16)

    ready_row(own[...], jnp.int32(0))
    ready_col(own[...], jnp.int32(0))
    acc_r[...] = jnp.zeros_like(acc_r)
    acc_c[...] = jnp.zeros_like(acc_c)
    upper = (lax.axis_index("tile") >= lax.axis_size("tile") // 2).astype(jnp.int32)
    shifts = [jnp.int32(0)] + [(me > team["team"]).astype(jnp.int32) for team in (far_team, near_team)]
    counts = [3 if group == (0, 0) else 2 if group == (0, HOPS) else 4 for group in ORDER]
    starts = [sum(counts[:number]) for number in range(len(ORDER))]
    units = sum(counts)
    first_use, last_use = {}, {}
    for (shard, place), start, count in zip(ORDER, starts, counts):
        used = [place - 1] if shard == 0 else [place - 1, place, HOPS - 1 + shard]
        for slot in used:
            if slot >= 0:
                first_use.setdefault(slot, start)
                last_use[slot] = start + count - 1

    for kind in (range(HOPS), range(HOPS, HOPS + 2)):
        taken = set()
        for slot in sorted(kind, key=lambda slot: -first_use[slot]):
            while first_use[slot] in taken:
                first_use[slot] -= 1
            taken.add(first_use[slot])

    def where(unit):
        shard, place, index = jnp.int32(0), jnp.int32(0), unit
        for (group_shard, group_place), start in zip(ORDER[1:], starts[1:]):
            here = unit >= start
            shard = jnp.where(here, group_shard, shard)
            place = jnp.where(here, group_place + shifts[group_shard], place)
            index = jnp.where(here, unit - start, index)
        row = lax.rem(index // 2, 2)
        col = 2 * place + lax.rem(index, 2)
        row = jnp.where(unit < 3, (unit == 1).astype(jnp.int32), row)
        col = jnp.where(unit < 3, (unit > 0).astype(jnp.int32), col)
        half = starts[ORDER.index((0, HOPS))]
        row = jnp.where(unit == half, upper, jnp.where(unit == half + 1, 1, row))
        col = jnp.where(unit == half, 2 * HOPS, jnp.where(unit == half + 1, 2 * HOPS + upper, col))
        return (shard * halves + row) * UNIT, col * UNIT, (unit >= 2).astype(F32)

    def distances(row, col, at):
        rows = row_x[pl.ds(pl.multiple_of(row + at, CHUNK), CHUNK), 0:DEPTH]
        return jnp.dot(rows, col_x[:, pl.ds(pl.multiple_of(col, UNIT), UNIT)], preferred_element_type=F32)

    def products(row, col, both, at):
        part = held[at // CHUNK]
        rows = pl.ds(pl.multiple_of(row + at, CHUNK), CHUNK)
        cols = pl.ds(pl.multiple_of(col, UNIT), UNIT)
        acc_c[:, cols] += jnp.dot(row_v[:, rows], part, preferred_element_type=F32)
        acc_r[:, rows] += both * lax.dot_general(
            col_v[:, cols], part, (((1,), (1,)), ((), ())), preferred_element_type=F32
        )

    def errands(unit):
        for number in range(units):
            giving = [slot for slot in last_use if last_use[slot] == number - 2]
            if giving:

                @pl.when(unit == number)
                def _(giving=giving):
                    for slot in giving:
                        give(slot).start()

        for slots, ready in ((range(HOPS), ready_col), (range(HOPS, HOPS + 2), ready_row)):
            due = [(slot, first_use[slot] - 1) for slot in slots]

            @pl.when(functools.reduce(jnp.logical_or, [unit == number for _, number in due]))
            def _(due=due, ready=ready, shift=1 if ready is ready_col else 1 - HOPS):
                slot = sum(jnp.where(unit == number, slot, 0) for slot, number in due)
                remote(own, came.at[slot], sends.at[slot], recvs.at[slot], far_team).wait_recv()
                ready(came[slot], slot + shift)

    def step(unit, carry):
        busy = [0, 0]
        for number in [first_use[slot] - 1 for slot in first_use] + [last_use[slot] + 2 for slot in last_use]:
            if number < units:
                busy[number // 32] |= 1 << number % 32
        low, high = [jnp.int32(word - (1 << 32) if word >> 31 else word) for word in busy]
        flags = jnp.where(unit < 32, low, high)

        @pl.when(jnp.bitwise_and(lax.shift_right_logical(flags, jnp.bitwise_and(unit, 31)), 1) == 1)
        def _():
            errands(unit)

        last, current, following = carry
        for at in range(0, UNIT, CHUNK):
            fresh = distances(following[0], following[1], at)
            if at == 0:
                products(*last, UNIT - CHUNK)
            else:
                products(*current, at - CHUNK)
            for line in range(0, CHUNK, 16):
                held[at // CHUNK, line : line + 16, :] = matern(small[at + line : at + line + 16, :])
            small[at : at + CHUNK, :] = fresh
        return current, following, where(jnp.minimum(unit + 2, units - 1))

    first = where(jnp.int32(0))
    held[...] = jnp.zeros_like(held)
    for at in range(0, UNIT, CHUNK):
        small[at : at + CHUNK, :] = distances(first[0], first[1], at)
    last, _, _ = lax.fori_loop(0, units, step, (first, first, where(jnp.int32(1))))
    products(*last, UNIT - CHUNK)
    for slot in last_use:
        if last_use[slot] > units - 3:
            give(slot).start()
    total = 0.5 * own[COORDS : COORDS + RHS, :] + acc_r[:, 0:size] + acc_c[:, 0:size]
    for slot in sorted(last_use, key=lambda slot: last_use[slot]):
        give(slot).wait_recv()
        total = total + back[slot]
    out_ref[...] = total
    for slot in range(6):
        fetch(slot).wait_send()
        give(slot).wait_send()


def vmem(count):
    return [pl.BlockSpec(memory_space=VMEM)] * count


def paired(pairing):
    def call(scales, points, vectors):
        size = points.shape[1]
        dma = pltpu.SemaphoreType.DMA
        return pl.pallas_call(
            functools.partial(kernel, pairing),
            out_shape=jax.ShapeDtypeStruct((RHS, size), F32),
            in_specs=[pl.BlockSpec(memory_space=pltpu.SMEM)] + [pl.BlockSpec(memory_space=pl.ANY)] * 2,
            out_specs=vmem(1)[0],
            scratch_shapes=[
                VMEM((COORDS + RHS, size), F32),
                VMEM((6, COORDS + RHS, size), F32),
                VMEM((UNIT, UNIT), F32),
                VMEM((UNIT // CHUNK, CHUNK, UNIT), BF16),
                VMEM((3 * size, 128), BF16),
                VMEM((DEPTH, (HOPS + 1) * size), BF16),
                VMEM((RHS, (HOPS + 1) * size), BF16),
                VMEM((RHS, 3 * size), BF16),
                VMEM((RHS, 3 * size), F32),
                VMEM((RHS, (HOPS + 1) * size), F32),
                VMEM((6, RHS, size), F32),
                dma((12,)),
                dma((12,)),
                dma((2,)),
            ],
            compiler_params=pltpu.CompilerParams(
                collective_id=pairing - 1, has_side_effects=True, vmem_limit_bytes=60 << 20
            ),
        )(scales, points, vectors)

    return call


def local(points, scales, vectors, plan):
    kernels = [paired(number) for number in range(1, 15)]
    return lax.switch(jnp.min(plan), [lambda *args: jnp.zeros(vectors.shape, F32)] + kernels, scales, points, vectors)


def solution(mesh):
    placed = (P(None, ("team", "tile")), P(), P(None, ("team", "tile")), P())
    return jax.shard_map(
        local, mesh=mesh, in_specs=placed, out_specs=P(None, ("team", "tile")), check_vma=False
    )
```

```python
import functools
import math

import jax
import jax.numpy as jnp
from jax import lax
from jax.experimental import pallas as pl
from jax.experimental.pallas import tpu as pltpu
from jax.sharding import PartitionSpec as P

MESH = pl.DeviceIdType.MESH
VMEM = pltpu.VMEM
F32 = jnp.float32
BF16 = jnp.bfloat16

SHRINK = math.sqrt(0.05)
RATE = -10.0 / math.log(2.0)
COORDS = 8
RHS = 16
DEPTH = 64
UNIT = 512
CHUNK = 256
HOPS = 4
ORDER = ((0, 0), (0, 1), (2, 0), (2, 1), (2, 2), (2, 3), (0, 3), (0, 4), (1, 2), (1, 3), (1, 1), (1, 0), (0, 2))
SENDS = (0, 5, 1, 4, 2, 3)


def tile_id(offset):
    count = lax.axis_size("tile")
    return {"tile": lax.rem(lax.axis_index("tile") + offset + count, count)}


def team_id(pairing):
    me = lax.axis_index("team")
    bits = lax.axis_size("team").bit_length() - 1
    other = me * 0
    for bit in range(bits):
        mine = lax.rem(me // (1 << bit), 2)
        other = other + (1 << bit) * (1 - mine if pairing >> bit & 1 else mine)
    return {"team": other}


def greet(friends):
    barrier = pltpu.get_barrier_semaphore()
    for friend in friends:
        pl.semaphore_signal(barrier, inc=1, device_id=friend, device_id_type=MESH)
    pl.semaphore_wait(barrier, len(friends))


def remote(src, dst, send, recv, target):
    return pltpu.make_async_remote_copy(
        src_ref=src, dst_ref=dst, send_sem=send, recv_sem=recv, device_id=target, device_id_type=MESH
    )


def pieces(value, count):
    out = []
    for _ in range(count):
        piece = value.astype(BF16).astype(F32)
        out.append(piece)
        value = value - piece
    return out


def split(shard, scales):
    scaled = shard[:COORDS] / scales * SHRINK
    one, two, three = pieces(scaled, 3)
    norm = jnp.sum(scaled * scaled, axis=0, keepdims=True)
    return one, two, three, pieces(norm, 3)


def place(parts, size):
    row = lax.broadcasted_iota(jnp.int32, (8, size), 0)
    out = jnp.zeros((8, size), F32)
    for at, part in enumerate(parts):
        out = jnp.where(row == at, part, out)
    return out


def col_operand(shard, scales):
    one, two, three, norms = split(shard, scales)
    unit = jnp.ones_like(norms[0])
    tail = place(norms + [unit] * 3, shard.shape[1])
    return jnp.concatenate([one, one, one, two, two, three, tail, jnp.zeros_like(tail)], 0).astype(BF16)


def row_operand(shard, scales):
    one, two, three, norms = split(shard, scales)
    unit = jnp.ones_like(norms[0])
    tail = place([unit] * 3 + norms, shard.shape[1])
    stack = [-2.0 * one, -2.0 * two, -2.0 * three, -2.0 * one, -2.0 * two, -2.0 * one, tail]
    stack += [jnp.zeros_like(tail)] * 9
    return jnp.concatenate(stack, 0).T


def matern(small):
    small = jnp.maximum(small, 1e-30)
    w = small * lax.rsqrt(small)
    return ((w * (w + 0.3) + 0.03) * jnp.exp2(w * RATE)).astype(BF16)


def kernel(
    pairing,
    scales_ref,
    points_ref,
    vectors_ref,
    out_ref,
    own,
    came,
    small,
    held,
    row_x,
    col_x,
    col_v,
    row_v,
    acc_r,
    acc_c,
    back,
    sends,
    recvs,
    locals_sem,
    lengths,
):
    size = own.shape[1]
    halves = size // UNIT
    far_team, near_team = team_id(15), team_id(pairing)
    me = lax.axis_index("team")
    loads = [
        pltpu.make_async_copy(points_ref, own.at[0:COORDS], locals_sem.at[0]),
        pltpu.make_async_copy(vectors_ref, own.at[COORDS : COORDS + RHS], locals_sem.at[1]),
    ]
    lengths_load = pltpu.make_async_copy(scales_ref, lengths, locals_sem.at[2])
    for load in loads + [lengths_load]:
        load.start()
    greet([tile_id(step) for step in range(1, lax.axis_size("tile"))] + [far_team, near_team])

    for load in loads:
        load.wait()

    def fetch(slot):
        target = tile_id(-1 - slot) if slot < HOPS else (far_team if slot == HOPS else near_team)
        return remote(own, came.at[slot], sends.at[slot], recvs.at[slot], target)

    def give(slot):
        target = tile_id(1 + slot) if slot < HOPS else (far_team if slot == HOPS else near_team)
        if slot < HOPS:
            src = acc_c.at[:, (slot + 1) * size : (slot + 2) * size]
        else:
            src = acc_r.at[:, (slot - 3) * size : (slot - 2) * size]
        return remote(src, back.at[slot], sends.at[6 + slot], recvs.at[6 + slot], target)

    for slot in SENDS:
        fetch(slot).start()

    line = lax.broadcasted_iota(jnp.int32, (COORDS, 1), 0)
    lengths_load.wait()
    scales = jnp.zeros((COORDS, 1), F32)
    for coord in range(COORDS):
        scales = jnp.where(line == coord, lengths[coord], scales)

    def ready_row(shard, row):
        at = pl.ds(pl.multiple_of(row * size, size), size)
        row_x[at, :] = row_operand(shard, scales).astype(BF16)
        row_v[:, at] = shard[COORDS:].astype(BF16)

    def ready_col(shard, hop):
        at = pl.ds(pl.multiple_of(hop * size, size), size)
        col_x[:, at] = col_operand(shard, scales)
        col_v[:, at] = shard[COORDS:].astype(BF16)

    ready_row(own[...], jnp.int32(0))
    ready_col(own[...], jnp.int32(0))
    acc_r[...] = jnp.zeros_like(acc_r)
    acc_c[...] = jnp.zeros_like(acc_c)
    upper = (lax.axis_index("tile") >= lax.axis_size("tile") // 2).astype(jnp.int32)
    shifts = [jnp.int32(0)] + [(me > team["team"]).astype(jnp.int32) for team in (far_team, near_team)]
    counts = [3 if group == (0, 0) else 2 if group == (0, HOPS) else 4 for group in ORDER]
    starts = [sum(counts[:number]) for number in range(len(ORDER))]
    units = sum(counts)
    first_use, last_use = {}, {}
    for (shard, place), start, count in zip(ORDER, starts, counts):
        used = [place - 1] if shard == 0 else [place - 1, place, HOPS - 1 + shard]
        for slot in used:
            if slot >= 0:
                first_use.setdefault(slot, start)
                last_use[slot] = start + count - 1

    for kind in (range(HOPS), range(HOPS, HOPS + 2)):
        taken = set()
        for slot in sorted(kind, key=lambda slot: -first_use[slot]):
            while first_use[slot] in taken:
                first_use[slot] -= 1
            taken.add(first_use[slot])

    def where(unit):
        shard, place, index = jnp.int32(0), jnp.int32(0), unit
        for (group_shard, group_place), start in zip(ORDER[1:], starts[1:]):
            here = unit >= start
            shard = jnp.where(here, group_shard, shard)
            place = jnp.where(here, group_place + shifts[group_shard], place)
            index = jnp.where(here, unit - start, index)
        row = lax.rem(index // 2, 2)
        col = 2 * place + lax.rem(index, 2)
        row = jnp.where(unit < 3, (unit == 1).astype(jnp.int32), row)
        col = jnp.where(unit < 3, (unit > 0).astype(jnp.int32), col)
        half = starts[ORDER.index((0, HOPS))]
        row = jnp.where(unit == half, upper, jnp.where(unit == half + 1, 1, row))
        col = jnp.where(unit == half, 2 * HOPS, jnp.where(unit == half + 1, 2 * HOPS + upper, col))
        return (shard * halves + row) * UNIT, col * UNIT, (unit >= 2).astype(F32)

    def distances(row, col, at):
        rows = row_x[pl.ds(pl.multiple_of(row + at, CHUNK), CHUNK), 0:DEPTH]
        return jnp.dot(rows, col_x[:, pl.ds(pl.multiple_of(col, UNIT), UNIT)], preferred_element_type=F32)

    def products(row, col, both, at):
        part = held[at // CHUNK]
        rows = pl.ds(pl.multiple_of(row + at, CHUNK), CHUNK)
        cols = pl.ds(pl.multiple_of(col, UNIT), UNIT)
        acc_c[:, cols] += jnp.dot(row_v[:, rows], part, preferred_element_type=F32)
        acc_r[:, rows] += both * lax.dot_general(
            col_v[:, cols], part, (((1,), (1,)), ((), ())), preferred_element_type=F32
        )

    def errands(unit):
        for number in range(units):
            giving = [slot for slot in last_use if last_use[slot] == number - 2]
            if giving:

                @pl.when(unit == number)
                def _(giving=giving):
                    for slot in giving:
                        give(slot).start()

        for slots, ready in ((range(HOPS), ready_col), (range(HOPS, HOPS + 2), ready_row)):
            due = [(slot, first_use[slot] - 1) for slot in slots]

            @pl.when(functools.reduce(jnp.logical_or, [unit == number for _, number in due]))
            def _(due=due, ready=ready, shift=1 if ready is ready_col else 1 - HOPS):
                slot = sum(jnp.where(unit == number, slot, 0) for slot, number in due)
                remote(own, came.at[slot], sends.at[slot], recvs.at[slot], far_team).wait_recv()
                ready(came[slot], slot + shift)

    def step(unit, carry):
        busy = [0, 0]
        for number in [first_use[slot] - 1 for slot in first_use] + [last_use[slot] + 2 for slot in last_use]:
            if number < units:
                busy[number // 32] |= 1 << number % 32
        low, high = [jnp.int32(word - (1 << 32) if word >> 31 else word) for word in busy]
        flags = jnp.where(unit < 32, low, high)

        @pl.when(jnp.bitwise_and(lax.shift_right_logical(flags, jnp.bitwise_and(unit, 31)), 1) == 1)
        def _():
            errands(unit)

        last, current, following = carry
        for at in range(0, UNIT, CHUNK):
            fresh = distances(following[0], following[1], at)
            if at == 0:
                products(*last, UNIT - CHUNK)
            else:
                products(*current, at - CHUNK)
            for line in range(0, CHUNK, 16):
                held[at // CHUNK, line : line + 16, :] = matern(small[at + line : at + line + 16, :])
            small[at : at + CHUNK, :] = fresh
        return current, following, where(jnp.minimum(unit + 2, units - 1))

    first = where(jnp.int32(0))
    held[...] = jnp.zeros_like(held)
    for at in range(0, UNIT, CHUNK):
        small[at : at + CHUNK, :] = distances(first[0], first[1], at)
    last, _, _ = lax.fori_loop(0, units, step, (first, first, where(jnp.int32(1))))
    products(*last, UNIT - CHUNK)
    for slot in last_use:
        if last_use[slot] > units - 3:
            give(slot).start()
    total = 0.5 * own[COORDS : COORDS + RHS, :] + acc_r[:, 0:size] + acc_c[:, 0:size]
    for slot in sorted(last_use, key=lambda slot: last_use[slot]):
        give(slot).wait_recv()
        total = total + back[slot]
    out_ref[...] = total
    for slot in range(6):
        fetch(slot).wait_send()
        give(slot).wait_send()


def vmem(count):
    return [pl.BlockSpec(memory_space=VMEM)] * count


def paired(pairing):
    def call(scales, points, vectors):
        size = points.shape[1]
        dma = pltpu.SemaphoreType.DMA
        return pl.pallas_call(
            functools.partial(kernel, pairing),
            out_shape=jax.ShapeDtypeStruct((RHS, size), F32),
            in_specs=[pl.BlockSpec(memory_space=pl.ANY)] * 3,
            out_specs=vmem(1)[0],
            scratch_shapes=[
                VMEM((COORDS + RHS, size), F32),
                VMEM((6, COORDS + RHS, size), F32),
                VMEM((UNIT, UNIT), F32),
                VMEM((UNIT // CHUNK, CHUNK, UNIT), BF16),
                VMEM((3 * size, 128), BF16),
                VMEM((DEPTH, (HOPS + 1) * size), BF16),
                VMEM((RHS, (HOPS + 1) * size), BF16),
                VMEM((RHS, 3 * size), BF16),
                VMEM((RHS, 3 * size), F32),
                VMEM((RHS, (HOPS + 1) * size), F32),
                VMEM((6, RHS, size), F32),
                dma((12,)),
                dma((12,)),
                dma((3,)),
                pltpu.SMEM((COORDS,), F32),
            ],
            compiler_params=pltpu.CompilerParams(
                collective_id=pairing - 1, has_side_effects=True, vmem_limit_bytes=60 << 20
            ),
        )(scales, points, vectors)

    return call


def local(points, scales, vectors, plan):
    kernels = [paired(number) for number in range(1, 15)]
    return lax.switch(jnp.min(plan), [lambda *args: jnp.zeros(vectors.shape, F32)] + kernels, scales, points, vectors)


def solution(mesh):
    placed = (P(None, ("team", "tile")), P(), P(None, ("team", "tile")), P())
    return jax.shard_map(
        local, mesh=mesh, in_specs=placed, out_specs=P(None, ("team", "tile")), check_vma=False
    )
```
